512 devices in a mesh: blk: 32 (over x, y, z_hi), grp: 16 (over z_lo, core).
Axes of the slice: x: 4, y: 4, z: 16 (z_hi: 2, z_lo: 8; z = z_hi * 8 + z_lo), core: 2. Of those that a mesh axis runs over, the one named last changes fastest.
Arguments:
- images: bfloat16 [131072, 1152], P(('blk', 'grp')), may hold values from -1.796875 to 1.796875
- texts: bfloat16 [131072, 1152], P(('blk', 'grp')), may hold values from -1.796875 to 1.796875
- log_temp: float32 [1], replicated, may hold values from -0.5 to 0.5
- bias: float32 [1], replicated, may hold values from -3 to 0
Outputs:
- image_grad: bfloat16 [131072, 1152], P(('blk', 'grp'))
- text_grad: bfloat16 [131072, 1152], P(('blk', 'grp'))
- bias_grad: float32 [1], replicated
- temp_grad: float32 [1], replicated
The draws below stay inside these ranges and needn't reach their ends.
All inputs are finite; a program needn't handle non-finite values.
Results may differ from the reference program's by a relative error of at most 0.0034.
Values may be sent and summed in bfloat16 or wider, within the bound.
No kernel may reach another device: no remote copies, remote signals or barrier semaphores. Data moves between devices by JAX's collectives and lax.ppermute only.
A program may use at most 64 MiB of HBM per device.

```python
import jax
import jax.numpy as jnp
from jax import lax

D = 1152
ROWS = 256
HOPS = 4
BATCH = 131072
N_BLK = 32
N_GRP = 16


def block_scale(own_key, shape, pieces, smallest, top_value):
    def one(dim, shards_of):
        steps = jax.random.uniform(jax.random.fold_in(jax.random.fold_in(own_key, 6), dim), (shards_of,), jnp.float32, smallest / len(pieces), top_value / len(pieces))
        return jnp.repeat(jnp.exp(steps), shape[dim] // shards_of).reshape((-1,) + (1,) * (len(shape) - dim - 1))

    level = one(*pieces[0])
    for cut in pieces[1:]:
        level = level * one(*cut)
    return level


def bell_draw(rng, extent, scale, reach, pieces=(), kind=jnp.bfloat16):
    array = scale * jax.random.normal(rng, extent, jnp.float32)
    if pieces:
        array = array * block_scale(rng, extent, pieces, -0.22, 0.18)
    return jnp.clip(array, -reach, reach).astype(kind)


def setup_inputs(seed: int = 0) -> dict:
    streams_of = jax.random.split(jax.random.key(seed), 5)
    return {
        "images": bell_draw(streams_of[0], (BATCH, D), 0.3, 1.796875, ((0, 512),)),
        "texts": bell_draw(streams_of[1], (BATCH, D), 0.3, 1.796875, ((0, 512),)),
        "log_temp": jnp.clip(jax.random.uniform(streams_of[2], (1,), jnp.float32, -0.5, 0.5), -0.5, 0.5),
        "bias": jnp.clip(jax.random.uniform(streams_of[3], (1,), jnp.float32, -3.0, 0.0), -3.0, 0.0),
    }


def reference(images, texts, log_temp, bias):
    logit_scale = jnp.exp(log_temp[0])
    logit_bias = bias[0]
    left = images.reshape(N_BLK, N_GRP, ROWS, D).astype(jnp.float32)
    right = texts.reshape(N_BLK, N_GRP, ROWS, D).astype(jnp.float32)
    diagonal = jnp.eye(ROWS, dtype=jnp.float32)
    grad_left = jnp.zeros(left.shape, jnp.float32)
    grad_right = jnp.zeros(right.shape, jnp.float32)
    bias_total = jnp.zeros((), jnp.float32)
    scale_total = jnp.zeros((), jnp.float32)
    for offset in range(-HOPS, HOPS + 1):
        moved = jnp.roll(right, -offset, axis=0)
        products = jnp.einsum('agrd,agsd->agrs', left, moved)
        logits = logit_scale * products + logit_bias
        slopes = jax.nn.sigmoid(logits)
        if offset == 0:
            slopes = slopes - diagonal
        bias_total = bias_total + jnp.sum(slopes)
        scale_total = scale_total + jnp.sum(slopes * (logits - logit_bias))
        half_slopes = lax.optimization_barrier(slopes.astype(jnp.bfloat16)).astype(jnp.float32)
        grad_left = grad_left + jnp.einsum('agrs,agsd->agrd', half_slopes, moved)
        part_right = jnp.einsum('agrs,agrd->agsd', half_slopes, left)
        grad_right = grad_right + jnp.roll(part_right, offset, axis=0)
    image_grad = (logit_scale * grad_left).astype(jnp.bfloat16).reshape(BATCH, D)
    text_grad = (logit_scale * grad_right).astype(jnp.bfloat16).reshape(BATCH, D)
    bias_grad = (bias_total / BATCH).reshape(1)
    temp_grad = (scale_total / BATCH).reshape(1)
    return image_grad, text_grad, bias_grad, temp_grad
```

```python
import jax
import jax.numpy as jnp
from jax import lax
from jax.experimental import pallas as pl
from jax.experimental.pallas import tpu as pltpu
from jax.sharding import PartitionSpec as P

F32, BF16 = jnp.float32, jnp.bfloat16
CHUNKS = 2
VMEM = pl.BlockSpec(memory_space=pltpu.VMEM)
SMEM = pl.BlockSpec(memory_space=pltpu.SMEM)
PARAMS = pltpu.CompilerParams(vmem_limit_bytes=48 * 1024 * 1024)


def dot(left, right, left_dim, right_dim):
    return lax.dot_general(
        left, right, (((left_dim,), (right_dim,)), ((), ())), preferred_element_type=F32
    )


def fold(tile):
    return jnp.sum(tile.reshape(-1, 8, tile.shape[-1]), axis=0)


def score(scalars, texts, images, on_diagonal):
    products = dot(texts, images, 1, 1)
    slopes = jax.nn.sigmoid(scalars[0] * products + scalars[1])
    if on_diagonal:
        rows = lax.broadcasted_iota(jnp.int32, slopes.shape, 0)
        columns = lax.broadcasted_iota(jnp.int32, slopes.shape, 1)
        slopes = slopes - jnp.where(rows == columns, 1.0, 0.0)
    return slopes.astype(BF16), fold(slopes), fold(slopes * products)


def own_kernel(scalars, texts, mine, ahead, behind, outer, inner, slopes_out, grad_out, inner_out, sums_out):
    bias_sum = scale_sum = grad = None
    for slot, images in enumerate((mine, ahead, behind, outer, inner)):
        half, bias_part, scale_part = score(scalars, texts[...], images[...], slot == 0)
        part = dot(half, images[...], 1, 0)
        if slot == 0:
            bias_sum, scale_sum, grad = bias_part, scale_part, part
        else:
            bias_sum, scale_sum, grad = bias_sum + bias_part, scale_sum + scale_part, grad + part
        if slot == 4:
            inner_out[...] = dot(half, texts[...], 0, 0).astype(BF16)
        else:
            slopes_out[slot] = half
    grad_out[...] = grad
    sums_out[0:8] = bias_sum
    sums_out[8:16] = scale_sum


def far_kernel(scalars, texts, mine, ahead, behind, outer, sums_in, slopes_out, grad_out, sums_out):
    bias_sum, scale_sum, grad = sums_in[0:8], sums_in[8:16], None
    for slot, images in enumerate((mine, ahead, behind, outer)):
        half, bias_part, scale_part = score(scalars, texts[...], images[...], False)
        part = dot(half, images[...], 1, 0)
        grad = part if grad is None else grad + part
        bias_sum, scale_sum = bias_sum + bias_part, scale_sum + scale_part
        slopes_out[slot] = half
    grad_out[...] = grad.astype(BF16)
    sums_out[0:8] = bias_sum
    sums_out[8:16] = scale_sum


def images_kernel(texts, own_slopes, *refs):
    far_texts, far_slopes = refs[:CHUNKS], refs[CHUNKS : 2 * CHUNKS]
    outs = refs[2 * CHUNKS :]
    for slot in (1, 2, 3, 0):
        grad = dot(own_slopes[slot], texts[...], 0, 0)
        for part, slopes in zip(far_texts, far_slopes, strict=True):
            grad = grad + dot(slopes[slot], part[...], 0, 0)
        outs[slot][...] = grad.astype(outs[slot].dtype)


def shape(rows, columns, kind):
    return jax.ShapeDtypeStruct((rows, columns), kind)


def cost(pairs, rows, width, moved):
    return pl.CostEstimate(flops=2 * pairs * rows * rows * width, bytes_accessed=moved, transcendentals=0)


def local(images, texts, log_temp, bias):
    rows, width = images.shape
    n_blk = lax.axis_size("blk")
    world = n_blk * lax.axis_size("grp")
    scale = jnp.exp(log_temp[0])
    scalars = jnp.stack([scale, bias[0]])
    block = rows * width * 2

    flip = [(s, s ^ 1) for s in range(n_blk)]

    def columns(count):
        return [(s, (s - 2 * count) % n_blk) for s in range(n_blk)]

    outward = [(s, (s - 4 * (1 - 2 * (s % 2))) % n_blk) for s in range(n_blk)]

    def back(pairs):
        return [(b, a) for a, b in pairs]

    part_rows = rows // CHUNKS
    far_texts = [
        lax.ppermute(texts[i * part_rows : (i + 1) * part_rows], "blk", flip) for i in range(CHUNKS)
    ]
    ways = (columns(1), columns(-1), outward, back(outward))
    ahead, behind, outer, inner = [lax.ppermute(images, "blk", way) for way in ways]

    own_slopes, text_own, inner_part, sums = pl.pallas_call(
        own_kernel,
        out_shape=(
            jax.ShapeDtypeStruct((4, rows, rows), BF16),
            shape(rows, width, F32),
            shape(rows, width, BF16),
            shape(16, rows, F32),
        ),
        in_specs=[SMEM] + [VMEM] * 6,
        out_specs=(VMEM,) * 4,
        compiler_params=PARAMS,
        cost_estimate=cost(11, rows, width, 10 * block),
        name="own_pairs",
    )(scalars, texts, images, ahead, behind, outer, inner)
    inner_back = lax.ppermute(inner_part, "blk", back(ways[3]))

    far_slopes, text_back = [], []
    for part in far_texts:
        slopes, grad, sums = pl.pallas_call(
            far_kernel,
            out_shape=(
                jax.ShapeDtypeStruct((4, part_rows, rows), BF16),
                shape(part_rows, width, BF16),
                shape(16, rows, F32),
            ),
            in_specs=[SMEM] + [VMEM] * 6,
            out_specs=(VMEM,) * 3,
            compiler_params=PARAMS,
            cost_estimate=cost(8 // CHUNKS, rows, width, 6 * block),
            name="far_pairs",
        )(scalars, part, images, ahead, behind, outer, sums)
        far_slopes.append(slopes)
        text_back.append(lax.ppermute(grad, "blk", flip))

    image_own, ahead_part, behind_part, outer_part = pl.pallas_call(
        images_kernel,
        out_shape=(shape(rows, width, F32),) + (shape(rows, width, BF16),) * 3,
        in_specs=[VMEM] * (2 + 2 * CHUNKS),
        out_specs=(VMEM,) * 4,
        compiler_params=PARAMS,
        cost_estimate=cost(8, rows, width, 8 * block),
        name="image_parts",
    )(texts, own_slopes, *far_texts, *far_slopes)
    image_back = [
        lax.ppermute(part, "blk", back(way))
        for part, way in zip((ahead_part, behind_part, outer_part), ways[:3], strict=True)
    ]

    totals = jnp.sum(sums.reshape(2, -1), axis=1)
    row = jnp.pad(totals, (0, 126)).reshape(1, 128)
    shared = lax.all_to_all(jnp.tile(row, (world, 1)), ("blk", "grp"), 0, 0, tiled=True)
    sums_all = jnp.sum(shared, axis=0)
    batch_rows = rows * world
    bias_grad = (sums_all[0] / batch_rows).reshape(1)
    temp_grad = (scale * sums_all[1] / batch_rows).reshape(1)

    image_sum = image_own + inner_back.astype(F32)
    for part in image_back:
        image_sum = image_sum + part.astype(F32)
    image_grad = (scale * image_sum).astype(BF16)
    text_grad = (scale * (text_own + jnp.concatenate(text_back, axis=0).astype(F32))).astype(BF16)
    return image_grad, text_grad, bias_grad, temp_grad


def solution(mesh):
    in_specs = (P(("blk", "grp"), None), P(("blk", "grp"), None), P(), P())
    out_specs = (P(("blk", "grp"), None), P(("blk", "grp"), None), P(), P())
    return jax.shard_map(local, mesh=mesh, in_specs=in_specs, out_specs=out_specs, check_vma=False)
```

```python
import jax
import jax.numpy as jnp
from jax import lax
from jax.experimental import pallas as pl
from jax.experimental.pallas import tpu as pltpu
from jax.sharding import Mesh
from jax.sharding import PartitionSpec as P

F32, BF16 = jnp.float32, jnp.bfloat16
VMEM = pl.BlockSpec(memory_space=pltpu.VMEM)
SMEM = pl.BlockSpec(memory_space=pltpu.SMEM)
PARAMS = pltpu.CompilerParams(vmem_limit_bytes=48 * 1024 * 1024)


def dot(left, right, left_dim, right_dim):
    return lax.dot_general(
        left, right, (((left_dim,), (right_dim,)), ((), ())), preferred_element_type=F32
    )


def fold(tile):
    return jnp.sum(tile.reshape(-1, 8, tile.shape[-1]), axis=0)


def score(scalars, texts, images, on_diagonal):
    products = dot(texts, images, 1, 1)
    slopes = jax.nn.sigmoid(scalars[0] * products + scalars[1])
    if on_diagonal:
        rows = lax.broadcasted_iota(jnp.int32, slopes.shape, 0)
        columns = lax.broadcasted_iota(jnp.int32, slopes.shape, 1)
        slopes = slopes - jnp.where(rows == columns, 1.0, 0.0)
    return slopes.astype(BF16), fold(slopes), fold(slopes * products)


def first_kernel(scalars, texts, mine, slopes_out, grad_out, sums_out, copy_out):
    half, bias_sum, scale_sum = score(scalars, texts[...], mine[...], True)
    slopes_out[...] = half
    grad_out[...] = dot(half, mine[...], 1, 0)
    copy_out[...] = mine[...]
    sums_out[0:8] = bias_sum
    sums_out[8:16] = scale_sum


def own_kernel(
    scalars, texts, ahead, behind, outer, inner, grad_in, sums_in, slopes_out, grad_out, inner_out, sums_out
):
    bias_sum, scale_sum, grad = sums_in[0:8], sums_in[8:16], grad_in[...]
    for slot, images in enumerate((ahead, behind, outer, inner)):
        half, bias_part, scale_part = score(scalars, texts[...], images[...], False)
        grad = grad + dot(half, images[...], 1, 0)
        bias_sum, scale_sum = bias_sum + bias_part, scale_sum + scale_part
        if slot == 3:
            inner_out[...] = dot(half, texts[...], 0, 0).astype(BF16)
        else:
            slopes_out[slot] = half
    grad_out[...] = grad
    sums_out[0:8] = bias_sum
    sums_out[8:16] = scale_sum


def lane_row(bias_sum, scale_sum):
    lane = lax.broadcasted_iota(jnp.int32, (1, 128), 1)
    return jnp.where(lane == 0, bias_sum, jnp.where(lane == 1, scale_sum, 0.0))


def far_kernel(scalars, texts, mine, ahead, behind, outer, sums, slopes_out, grad_out, row_out):
    bias_sum, scale_sum, grad = sums[0:8], sums[8:16], None
    for slot, images in enumerate((mine, ahead, behind, outer)):
        half, bias_part, scale_part = score(scalars, texts[...], images[...], False)
        part = dot(half, images[...], 1, 0)
        grad = part if grad is None else grad + part
        bias_sum, scale_sum = bias_sum + bias_part, scale_sum + scale_part
        slopes_out[slot] = half
    grad_out[...] = grad.astype(BF16)
    row_out[...] = jnp.broadcast_to(lane_row(jnp.sum(bias_sum), jnp.sum(scale_sum)), row_out.shape)


def images_kernel(
    texts, first_slopes, own_slopes, far_texts, far_slopes, rows, mine_out, ahead_out, behind_out, outer_out, row_out
):
    for slot, out in ((1, ahead_out), (2, behind_out), (3, outer_out), (0, mine_out)):
        own = first_slopes[...] if slot == 0 else own_slopes[slot - 1]
        grad = dot(own, texts[...], 0, 0) + dot(far_slopes[slot], far_texts[...], 0, 0)
        out[...] = grad.astype(out.dtype)
    row_out[...] = jnp.broadcast_to(jnp.sum(rows[...], axis=0, keepdims=True), row_out.shape)


def shape(rows, columns, kind):
    return jax.ShapeDtypeStruct((rows, columns), kind)


def cost(moved):
    return pl.CostEstimate(flops=0, bytes_accessed=moved, transcendentals=0)


def call(kernel, name, outs, in_smem, args, moved):
    return pl.pallas_call(
        kernel,
        out_shape=outs,
        in_specs=[SMEM] * in_smem + [VMEM] * (len(args) - in_smem),
        out_specs=(VMEM,) * len(outs),
        compiler_params=PARAMS,
        cost_estimate=pl.CostEstimate(flops=0, bytes_accessed=moved, transcendentals=0),
        name=name,
    )(*args)


def local(images, texts, log_temp, bias):
    rows, width = images.shape
    columns_count, halves = lax.axis_size(("x", "y")), lax.axis_size("half")
    in_column = halves * lax.axis_size("grp")
    stops = columns_count * halves
    scale = jnp.exp(log_temp[0])
    scalars = jnp.stack([scale, bias[0]])
    block = rows * width * 2

    def moved(value, pairs):
        return lax.ppermute(value, ("x", "y", "half"), pairs)

    def columns(count):
        return [(s, (s - 2 * count) % stops) for s in range(stops)]

    def back(pairs):
        return [(b, a) for a, b in pairs]

    flip = [(s, s ^ 1) for s in range(stops)]
    outward = [(s, (s - 4 * (1 - 2 * (s % 2))) % stops) for s in range(stops)]
    ways = (columns(1), columns(-1), outward, back(outward))

    far_texts = moved(texts, flip)
    first_slopes, text_first, sums, images_too = call(
        first_kernel,
        "first_pair",
        (shape(rows, rows, BF16), shape(rows, width, F32), shape(16, rows, F32), shape(rows, width, BF16)),
        1,
        (scalars, texts, images),
        100 * block,
    )
    near = [moved(images_too, way) for way in ways]
    far_texts, *near = lax.optimization_barrier((far_texts, *near))
    own_slopes, text_own, inner_part, sums = call(
        own_kernel,
        "own_pairs",
        (
            jax.ShapeDtypeStruct((3, rows, rows), BF16),
            shape(rows, width, F32),
            shape(rows, width, BF16),
            shape(16, rows, F32),
        ),
        1,
        (scalars, texts, *near, text_first, sums),
        block,
    )
    inner_back = moved(inner_part, back(ways[3]))
    far_slopes, far_grad, row_copies = call(
        far_kernel,
        "far_pairs",
        (
            jax.ShapeDtypeStruct((4, rows, rows), BF16),
            shape(rows, width, BF16),
            shape(columns_count, 128, F32),
        ),
        1,
        (scalars, far_texts, images, *near[:3], sums),
        block,
    )
    text_back = moved(far_grad, flip)
    level_rows = lax.all_to_all(row_copies, ("x", "y"), 0, 0, tiled=True)
    image_own, *image_parts, row_copies = call(
        images_kernel,
        "image_parts",
        (shape(rows, width, F32),) + (shape(rows, width, BF16),) * 3 + (shape(in_column, 128, F32),),
        0,
        (texts, first_slopes, own_slopes, far_texts, far_slopes, level_rows),
        block,
    )
    image_back = [moved(part, back(way)) for part, way in zip(image_parts, ways[:3], strict=True)]
    row_copies, text_back = lax.optimization_barrier((row_copies, text_back))
    sums_all = jnp.sum(lax.all_to_all(row_copies, ("half", "grp"), 0, 0, tiled=True), axis=0)

    batch_rows = rows * columns_count * in_column
    bias_grad = (sums_all[0] / batch_rows).reshape(1)
    temp_grad = (scale * sums_all[1] / batch_rows).reshape(1)
    image_sum = image_own + inner_back.astype(F32)
    for part in image_back:
        image_sum = image_sum + part.astype(F32)
    image_grad = (scale * image_sum).astype(BF16)
    text_grad = (scale * (text_own + text_back.astype(F32))).astype(BF16)
    return image_grad, text_grad, bias_grad, temp_grad


def solution(mesh):
    x_y_half = (4, 4, 2)
    fine = Mesh(mesh.devices.reshape(*x_y_half, -1), ("x", "y", "half", "grp"))
    split = P(("x", "y", "half", "grp"), None)
    return jax.shard_map(
        local, mesh=fine, in_specs=(split, split, P(), P()), out_specs=(split, split, P(), P()), check_vma=False
    )
```

```python
import jax
import jax.numpy as jnp
from jax import lax
from jax.experimental import pallas as pl
from jax.experimental.pallas import tpu as pltpu
from jax.sharding import Mesh
from jax.sharding import PartitionSpec as P

F32, BF16 = jnp.float32, jnp.bfloat16
VMEM = pl.BlockSpec(memory_space=pltpu.VMEM)
SMEM = pl.BlockSpec(memory_space=pltpu.SMEM)
PARAMS = pltpu.CompilerParams(vmem_limit_bytes=48 * 1024 * 1024)


def dot(left, right, left_dim, right_dim):
    return lax.dot_general(
        left, right, (((left_dim,), (right_dim,)), ((), ())), preferred_element_type=F32
    )


def fold(tile):
    return jnp.sum(tile.reshape(-1, 8, tile.shape[-1]), axis=0)


def score(scalars, texts, images, on_diagonal):
    products = dot(texts, images, 1, 1)
    slopes = jax.nn.sigmoid(scalars[0] * products + scalars[1])
    if on_diagonal:
        rows = lax.broadcasted_iota(jnp.int32, slopes.shape, 0)
        columns = lax.broadcasted_iota(jnp.int32, slopes.shape, 1)
        slopes = slopes - jnp.where(rows == columns, 1.0, 0.0)
    return slopes.astype(BF16), fold(slopes), fold(slopes * products)


def first_kernel(scalars, texts, mine, slopes_out, grad_out, sums_out):
    half, bias_sum, scale_sum = score(scalars, texts[...], mine[...], True)
    slopes_out[...] = half
    grad_out[...] = dot(half, mine[...], 1, 0)
    sums_out[0:8] = bias_sum
    sums_out[8:16] = scale_sum


def own_kernel(scalars, texts, *refs):
    images, (grad_in, sums_in, slopes_out, grad_out, row_out) = refs[:4], refs[4:]
    bias_sum, scale_sum, grad = sums_in[0:8], sums_in[8:16], grad_in[...]
    for slot, near in enumerate(images):
        half, bias_part, scale_part = score(scalars, texts[...], near[...], False)
        grad = grad + dot(half, near[...], 1, 0)
        bias_sum, scale_sum = bias_sum + bias_part, scale_sum + scale_part
        slopes_out[slot] = half
    grad_out[...] = grad
    row_out[...] = jnp.broadcast_to(lane_row(jnp.sum(bias_sum), jnp.sum(scale_sum)), row_out.shape)


def lane_row(bias_sum, scale_sum):
    lane = lax.broadcasted_iota(jnp.int32, (1, 128), 1)
    return jnp.where(lane == 0, bias_sum, jnp.where(lane == 1, scale_sum, 0.0))


def far_kernel(scalars, texts, mine, ahead, behind, ahead_2, behind_2, sums, slopes_out, grad_out, sums_out):
    bias_sum, scale_sum, grad = sums[0:8], sums[8:16], None
    outer = jnp.where(scalars[2] > 0.5, ahead_2[...], behind_2[...])
    for slot, images in enumerate((mine[...], ahead[...], behind[...], outer)):
        half, bias_part, scale_part = score(scalars, texts[...], images, False)
        part = dot(half, images, 1, 0)
        grad = part if grad is None else grad + part
        bias_sum, scale_sum = bias_sum + bias_part, scale_sum + scale_part
        if slot < 3:
            slopes_out[slot] = half
        else:
            slopes_out[3] = jnp.where(scalars[2] > 0.5, half, jnp.zeros_like(half))
            slopes_out[4] = jnp.where(scalars[2] > 0.5, jnp.zeros_like(half), half)
    grad_out[...] = grad.astype(BF16)
    sums_out[0:8] = bias_sum
    sums_out[8:16] = scale_sum


def images_kernel(texts, first_slopes, own_slopes, far_texts, far_slopes, rows, *outs):
    for slot in (3, 4, 1, 2, 0):
        own = first_slopes[...] if slot == 0 else own_slopes[slot - 1]
        grad = dot(own, texts[...], 0, 0) + dot(far_slopes[slot], far_texts[...], 0, 0)
        outs[slot][...] = grad.astype(outs[slot].dtype)
    outs[5][...] = jnp.broadcast_to(jnp.sum(rows[...], axis=0, keepdims=True), outs[5].shape)


def shape(rows, columns, kind):
    return jax.ShapeDtypeStruct((rows, columns), kind)


def cost(moved):
    return pl.CostEstimate(flops=0, bytes_accessed=moved, transcendentals=0)


def call(kernel, name, outs, in_smem, args, moved):
    return pl.pallas_call(
        kernel,
        out_shape=outs,
        in_specs=[SMEM] * in_smem + [VMEM] * (len(args) - in_smem),
        out_specs=(VMEM,) * len(outs),
        compiler_params=PARAMS,
        cost_estimate=pl.CostEstimate(flops=0, bytes_accessed=moved, transcendentals=0),
        name=name,
    )(*args)


def local(images, texts, log_temp, bias):
    rows, width = images.shape
    columns_count, halves = lax.axis_size(("x", "y")), lax.axis_size("half")
    in_column = halves * lax.axis_size("grp")
    stops = columns_count * halves
    scale = jnp.exp(log_temp[0])
    first_half = (lax.axis_index("half") == 0).astype(F32)
    scalars = jnp.stack([scale, bias[0], first_half])
    block = rows * width * 2

    def moved(value, pairs):
        return lax.ppermute(value, ("x", "y", "half"), pairs)

    def columns(count):
        return [(s, (s - 2 * count) % stops) for s in range(stops)]

    def back(pairs):
        return [(b, a) for a, b in pairs]

    flip = [(s, s ^ 1) for s in range(stops)]
    ways = (columns(1), columns(-1), columns(2), columns(-2))

    far_texts = moved(texts, flip)
    ahead, behind = moved(images, ways[0]), moved(images, ways[1])
    ahead_2, behind_2 = moved(images, ways[2]), moved(images, ways[3])
    first_slopes, text_first, sums = call(
        first_kernel,
        "first_pair",
        (shape(rows, rows, BF16), shape(rows, width, F32), shape(16, rows, F32)),
        1,
        (scalars, texts, images),
        100 * block,
    )
    far_texts, ahead, behind, ahead_2, behind_2 = lax.optimization_barrier(
        (far_texts, ahead, behind, ahead_2, behind_2)
    )
    near = (ahead, behind, ahead_2, behind_2)
    far_slopes, far_grad, sums = call(
        far_kernel,
        "far_pairs",
        (jax.ShapeDtypeStruct((5, rows, rows), BF16), shape(rows, width, BF16), shape(16, rows, F32)),
        1,
        (scalars, far_texts, images, *near, sums),
        block,
    )
    text_back = moved(far_grad, flip)
    own_slopes, text_own, row_copies = call(
        own_kernel,
        "own_pairs",
        (
            jax.ShapeDtypeStruct((4, rows, rows), BF16),
            shape(rows, width, F32),
            shape(columns_count, 128, F32),
        ),
        1,
        (scalars, texts, *near, text_first, sums),
        block,
    )
    level_rows = lax.all_to_all(row_copies, ("x", "y"), 0, 0, tiled=True)
    image_own, *image_parts, row_copies = call(
        images_kernel,
        "image_parts",
        (shape(rows, width, F32),) + (shape(rows, width, BF16),) * 4 + (shape(in_column, 128, F32),),
        0,
        (texts, first_slopes, own_slopes, far_texts, far_slopes, level_rows),
        block,
    )
    image_back = [moved(part, back(way)) for part, way in zip(image_parts, ways, strict=True)]
    row_copies, text_back = lax.optimization_barrier((row_copies, text_back))
    sums_all = jnp.sum(lax.all_to_all(row_copies, ("half", "grp"), 0, 0, tiled=True), axis=0)

    batch_rows = rows * columns_count * in_column
    bias_grad = (sums_all[0] / batch_rows).reshape(1)
    temp_grad = (scale * sums_all[1] / batch_rows).reshape(1)
    image_sum = image_own
    for part in image_back:
        image_sum = image_sum + part.astype(F32)
    image_grad = (scale * image_sum).astype(BF16)
    text_grad = (scale * (text_own + text_back.astype(F32))).astype(BF16)
    return image_grad, text_grad, bias_grad, temp_grad


def solution(mesh):
    x_y_half = (4, 4, 2)
    fine = Mesh(mesh.devices.reshape(*x_y_half, -1), ("x", "y", "half", "grp"))
    split = P(("x", "y", "half", "grp"), None)
    return jax.shard_map(
        local, mesh=fine, in_specs=(split, split, P(), P()), out_specs=(split, split, P(), P()), check_vma=False
    )
```

```python
import jax
import jax.numpy as jnp
from jax import lax
from jax.experimental import pallas as pl
from jax.experimental.pallas import tpu as pltpu
from jax.sharding import Mesh
from jax.sharding import PartitionSpec as P

F32, BF16 = jnp.float32, jnp.bfloat16
VMEM = pl.BlockSpec(memory_space=pltpu.VMEM)
SMEM = pl.BlockSpec(memory_space=pltpu.SMEM)
PARAMS = pltpu.CompilerParams(vmem_limit_bytes=48 * 1024 * 1024)


def dot(left, right, left_dim, right_dim):
    return lax.dot_general(
        left, right, (((left_dim,), (right_dim,)), ((), ())), preferred_element_type=F32
    )


def fold(tile):
    return jnp.sum(tile.reshape(-1, 8, tile.shape[-1]), axis=0)


def score(scalars, texts, images, on_diagonal):
    products = dot(texts, images, 1, 1)
    slopes = jax.nn.sigmoid(scalars[0] * products + scalars[1])
    if on_diagonal:
        rows = lax.broadcasted_iota(jnp.int32, slopes.shape, 0)
        columns = lax.broadcasted_iota(jnp.int32, slopes.shape, 1)
        slopes = slopes - jnp.where(rows == columns, 1.0, 0.0)
    return slopes.astype(BF16), fold(slopes), fold(slopes * products)


def first_kernel(scalars, texts, mine, slopes_out, grad_out, sums_out):
    half, bias_sum, scale_sum = score(scalars, texts[...], mine[...], True)
    slopes_out[...] = half
    grad_out[...] = dot(half, mine[...], 1, 0)
    sums_out[0:8] = bias_sum
    sums_out[8:16] = scale_sum


def own_kernel(first_grad, own_slopes, ahead, behind, outer, inner, grad_out):
    grad = first_grad[...]
    for slot, images in enumerate((ahead, behind, outer, inner)):
        grad = grad + dot(own_slopes[slot], images[...], 1, 0)
    grad_out[...] = grad


def lane_row(bias_sum, scale_sum):
    lane = lax.broadcasted_iota(jnp.int32, (1, 128), 1)
    return jnp.where(lane == 0, bias_sum, jnp.where(lane == 1, scale_sum, 0.0))


def far_kernel(scalars, texts, mine, ahead, behind, outer, sums, slopes_out, grad_out, sums_out):
    bias_sum, scale_sum, grad = sums[0:8], sums[8:16], None
    for slot, images in enumerate((mine, ahead, behind, outer)):
        half, bias_part, scale_part = score(scalars, texts[...], images[...], False)
        part = dot(half, images[...], 1, 0)
        grad = part if grad is None else grad + part
        bias_sum, scale_sum = bias_sum + bias_part, scale_sum + scale_part
        slopes_out[slot] = half
    grad_out[...] = grad.astype(BF16)
    sums_out[0:8] = bias_sum
    sums_out[8:16] = scale_sum


def images_kernel(
    scalars, texts, ahead, behind, outer, inner, sums, first_slopes, far_texts, far_slopes, own_out, row_out, *outs
):
    bias_sum, scale_sum = sums[0:8], sums[8:16]
    near = (None, ahead, behind, outer, inner)
    for slot in (3, 4, 1, 2, 0):
        if slot == 0:
            half = first_slopes[...]
        else:
            half, bias_part, scale_part = score(scalars, texts[...], near[slot][...], False)
            bias_sum, scale_sum = bias_sum + bias_part, scale_sum + scale_part
            own_out[slot - 1] = half
        grad = dot(half, texts[...], 0, 0)
        if slot < 4:
            grad = grad + dot(far_slopes[slot], far_texts[...], 0, 0)
        outs[slot][...] = grad.astype(outs[slot].dtype)
    row_out[...] = jnp.broadcast_to(lane_row(jnp.sum(bias_sum), jnp.sum(scale_sum)), row_out.shape)


def column_kernel(rows, *refs):
    refs[-1][...] = jnp.broadcast_to(jnp.sum(rows[...], axis=0, keepdims=True), refs[-1].shape)


def shape(rows, columns, kind):
    return jax.ShapeDtypeStruct((rows, columns), kind)


def cost(moved):
    return pl.CostEstimate(flops=0, bytes_accessed=moved, transcendentals=0)


def call(kernel, name, outs, in_smem, args, moved):
    return pl.pallas_call(
        kernel,
        out_shape=outs,
        in_specs=[SMEM] * in_smem + [VMEM] * (len(args) - in_smem),
        out_specs=(VMEM,) * len(outs),
        compiler_params=PARAMS,
        cost_estimate=pl.CostEstimate(flops=0, bytes_accessed=moved, transcendentals=0),
        name=name,
    )(*args)


def local(images, texts, log_temp, bias):
    rows, width = images.shape
    columns_count, halves = lax.axis_size(("x", "y")), lax.axis_size("half")
    in_column = halves * lax.axis_size("grp")
    stops = columns_count * halves
    scale = jnp.exp(log_temp[0])
    scalars = jnp.stack([scale, bias[0]])
    block = rows * width * 2

    def moved(value, pairs):
        return lax.ppermute(value, ("x", "y", "half"), pairs)

    def columns(count):
        return [(s, (s - 2 * count) % stops) for s in range(stops)]

    def back(pairs):
        return [(b, a) for a, b in pairs]

    flip = [(s, s ^ 1) for s in range(stops)]
    outward = [(s, (s - 4 * (1 - 2 * (s % 2))) % stops) for s in range(stops)]
    ways = (columns(1), columns(-1), outward, back(outward))

    far_texts = moved(texts, flip)
    ahead, behind, outer, inner = [moved(images, way) for way in ways]
    first_slopes, text_first, sums = call(
        first_kernel,
        "first_pair",
        (shape(rows, rows, BF16), shape(rows, width, F32), shape(16, rows, F32)),
        1,
        (scalars, texts, images),
        100 * block,
    )
    far_texts, ahead, behind, outer = lax.optimization_barrier((far_texts, ahead, behind, outer))
    near = (ahead, behind, outer, inner)
    far_slopes, far_grad, sums = call(
        far_kernel,
        "far_pairs",
        (jax.ShapeDtypeStruct((4, rows, rows), BF16), shape(rows, width, BF16), shape(16, rows, F32)),
        1,
        (scalars, far_texts, images, *near[:3], sums),
        block,
    )
    text_back = moved(far_grad, flip)
    own_slopes, row_copies, image_own, *image_parts = call(
        images_kernel,
        "image_parts",
        (jax.ShapeDtypeStruct((4, rows, rows), BF16), shape(in_column, 128, F32), shape(rows, width, F32))
        + (shape(rows, width, BF16),) * 4,
        1,
        (scalars, texts, *near, sums, first_slopes, far_texts, far_slopes),
        block,
    )
    image_back = [moved(part, back(way)) for part, way in zip(image_parts, ways, strict=True)]
    own_slopes, text_first, image_own = lax.optimization_barrier((own_slopes, text_first, image_own))
    (text_own,) = call(
        own_kernel, "own_texts", (shape(rows, width, F32),), 0, (text_first, own_slopes, *near), block
    )
    row_copies, text_own = lax.optimization_barrier((row_copies, text_own))
    column_rows = lax.all_to_all(row_copies, ("half", "grp"), 0, 0, tiled=True)
    row_copies = pl.pallas_call(
        column_kernel,
        out_shape=shape(columns_count, 128, F32),
        in_specs=[VMEM] * 3,
        out_specs=VMEM,
        compiler_params=PARAMS,
        name="column_sums",
    )(column_rows, text_back, image_back[0])
    sums_all = jnp.sum(lax.all_to_all(row_copies, ("x", "y"), 0, 0, tiled=True), axis=0)

    batch_rows = rows * columns_count * in_column
    bias_grad = (sums_all[0] / batch_rows).reshape(1)
    temp_grad = (scale * sums_all[1] / batch_rows).reshape(1)
    image_sum = image_own
    for part in image_back:
        image_sum = image_sum + part.astype(F32)
    text_grad = (scale * (text_own + text_back.astype(F32))).astype(BF16)
    image_grad = (scale * image_sum).astype(BF16)
    return image_grad, text_grad, bias_grad, temp_grad


def solution(mesh):
    x_y_half = (4, 4, 2)
    fine = Mesh(mesh.devices.reshape(*x_y_half, -1), ("x", "y", "half", "grp"))
    split = P(("x", "y", "half", "grp"), None)
    return jax.shard_map(
        local, mesh=fine, in_specs=(split, split, P(), P()), out_specs=(split, split, P(), P()), check_vma=False
    )
```

```python
import jax
import jax.numpy as jnp
from jax import lax
from jax.experimental import pallas as pl
from jax.experimental.pallas import tpu as pltpu
from jax.sharding import Mesh
from jax.sharding import PartitionSpec as P

F32, BF16 = jnp.float32, jnp.bfloat16
VMEM = pl.BlockSpec(memory_space=pltpu.VMEM)
SMEM = pl.BlockSpec(memory_space=pltpu.SMEM)
PARAMS = pltpu.CompilerParams(vmem_limit_bytes=48 * 1024 * 1024)


def dot(left, right, left_dim, right_dim):
    return lax.dot_general(
        left, right, (((left_dim,), (right_dim,)), ((), ())), preferred_element_type=F32
    )


def fold(tile):
    return jnp.sum(tile.reshape(-1, 8, tile.shape[-1]), axis=0)


def score(scalars, texts, images, on_diagonal):
    products = dot(texts, images, 1, 1)
    slopes = jax.nn.sigmoid(scalars[0] * products + scalars[1])
    if on_diagonal:
        rows = lax.broadcasted_iota(jnp.int32, slopes.shape, 0)
        columns = lax.broadcasted_iota(jnp.int32, slopes.shape, 1)
        slopes = slopes - jnp.where(rows == columns, 1.0, 0.0)
    return slopes.astype(BF16), fold(slopes), fold(slopes * products)


def first_kernel(scalars, texts, mine, slopes_out, grad_out, sums_out):
    half, bias_sum, scale_sum = score(scalars, texts[...], mine[...], True)
    slopes_out[...] = half
    grad_out[...] = dot(half, mine[...], 1, 0)
    sums_out[0:8] = bias_sum
    sums_out[8:16] = scale_sum


def own_kernel(first_grad, own_slopes, ahead, behind, outer, inner, grad_out):
    grad = first_grad[...]
    for slot, images in enumerate((ahead, behind, outer, inner)):
        grad = grad + dot(own_slopes[slot], images[...], 1, 0)
    grad_out[...] = grad


def lane_row(bias_sum, scale_sum):
    lane = lax.broadcasted_iota(jnp.int32, (1, 128), 1)
    return jnp.where(lane == 0, bias_sum, jnp.where(lane == 1, scale_sum, 0.0))


def far_kernel(scalars, texts, mine, ahead, behind, outer, sums, slopes_out, grad_out, sums_out):
    bias_sum, scale_sum, grad = sums[0:8], sums[8:16], None
    for slot, images in enumerate((mine, ahead, behind, outer)):
        half, bias_part, scale_part = score(scalars, texts[...], images[...], False)
        part = dot(half, images[...], 1, 0)
        grad = part if grad is None else grad + part
        bias_sum, scale_sum = bias_sum + bias_part, scale_sum + scale_part
        slopes_out[slot] = half
    grad_out[...] = grad.astype(BF16)
    sums_out[0:8] = bias_sum
    sums_out[8:16] = scale_sum


def images_kernel(
    scalars, texts, ahead, behind, outer, inner, sums, first_slopes, far_texts, far_slopes, own_out, row_out, *outs
):
    bias_sum, scale_sum = sums[0:8], sums[8:16]
    near = (None, ahead, behind, outer, inner)
    for slot in (3, 4, 1, 2, 0):
        if slot == 0:
            half = first_slopes[...]
        else:
            half, bias_part, scale_part = score(scalars, texts[...], near[slot][...], False)
            bias_sum, scale_sum = bias_sum + bias_part, scale_sum + scale_part
            own_out[slot - 1] = half
        grad = dot(half, texts[...], 0, 0)
        if slot < 4:
            grad = grad + dot(far_slopes[slot], far_texts[...], 0, 0)
        outs[slot][...] = grad.astype(outs[slot].dtype)
    row_out[...] = jnp.broadcast_to(lane_row(jnp.sum(bias_sum), jnp.sum(scale_sum)), row_out.shape)


def column_kernel(rows, *refs):
    refs[-1][...] = jnp.broadcast_to(jnp.sum(rows[...], axis=0, keepdims=True), refs[-1].shape)


def shape(rows, columns, kind):
    return jax.ShapeDtypeStruct((rows, columns), kind)


def cost(moved):
    return pl.CostEstimate(flops=0, bytes_accessed=moved, transcendentals=0)


def call(kernel, name, outs, in_smem, args, moved):
    return pl.pallas_call(
        kernel,
        out_shape=outs,
        in_specs=[SMEM] * in_smem + [VMEM] * (len(args) - in_smem),
        out_specs=(VMEM,) * len(outs),
        compiler_params=PARAMS,
        cost_estimate=pl.CostEstimate(flops=0, bytes_accessed=moved, transcendentals=0),
        name=name,
    )(*args)


def local(images, texts, log_temp, bias):
    rows, width = images.shape
    columns_count, halves = lax.axis_size(("x", "y")), lax.axis_size("half")
    in_column = halves * lax.axis_size("grp")
    stops = columns_count * halves
    scale = jnp.exp(log_temp[0])
    scalars = jnp.stack([scale, bias[0]])
    block = rows * width * 2

    def moved(value, pairs):
        return lax.ppermute(value, ("x", "y", "half"), pairs)

    def columns(count):
        return [(s, (s - 2 * count) % stops) for s in range(stops)]

    def back(pairs):
        return [(b, a) for a, b in pairs]

    flip = [(s, s ^ 1) for s in range(stops)]
    outward = [(s, (s - 4 * (1 - 2 * (s % 2))) % stops) for s in range(stops)]
    ways = (columns(1), columns(-1), outward, back(outward))

    far_texts = moved(texts, flip)
    ahead, behind, outer, inner = [moved(images, way) for way in ways]
    first_slopes, text_first, sums = call(
        first_kernel,
        "first_pair",
        (shape(rows, rows, BF16), shape(rows, width, F32), shape(16, rows, F32)),
        1,
        (scalars, texts, images),
        100 * block,
    )
    far_texts, outer, ahead, behind = lax.optimization_barrier((far_texts, outer, ahead, behind))
    near = (ahead, behind, outer, inner)
    far_slopes, far_grad, sums = call(
        far_kernel,
        "far_pairs",
        (jax.ShapeDtypeStruct((4, rows, rows), BF16), shape(rows, width, BF16), shape(16, rows, F32)),
        1,
        (scalars, far_texts, images, *near[:3], sums),
        block,
    )
    text_back = moved(far_grad, flip)
    own_slopes, row_copies, image_own, *image_parts = call(
        images_kernel,
        "image_parts",
        (jax.ShapeDtypeStruct((4, rows, rows), BF16), shape(in_column, 128, F32), shape(rows, width, F32))
        + (shape(rows, width, BF16),) * 4,
        1,
        (scalars, texts, *near, sums, first_slopes, far_texts, far_slopes),
        block,
    )
    image_back = [moved(part, back(way)) for part, way in zip(image_parts, ways, strict=True)]
    own_slopes, text_first, image_own = lax.optimization_barrier((own_slopes, text_first, image_own))
    (text_own,) = call(
        own_kernel, "own_texts", (shape(rows, width, F32),), 0, (text_first, own_slopes, *near), block
    )
    row_copies, text_own = lax.optimization_barrier((row_copies, text_own))
    column_rows = lax.all_to_all(row_copies, ("half", "grp"), 0, 0, tiled=True)
    row_copies = pl.pallas_call(
        column_kernel,
        out_shape=shape(columns_count, 128, F32),
        in_specs=[VMEM] * 3,
        out_specs=VMEM,
        compiler_params=PARAMS,
        name="column_sums",
    )(column_rows, text_back, image_back[0])
    sums_all = jnp.sum(lax.all_to_all(row_copies, ("x", "y"), 0, 0, tiled=True), axis=0)

    batch_rows = rows * columns_count * in_column
    bias_grad = (sums_all[0] / batch_rows).reshape(1)
    temp_grad = (scale * sums_all[1] / batch_rows).reshape(1)
    image_sum = image_own
    for part in image_back:
        image_sum = image_sum + part.astype(F32)
    text_grad = (scale * (text_own + text_back.astype(F32))).astype(BF16)
    image_grad = (scale * image_sum).astype(BF16)
    return image_grad, text_grad, bias_grad, temp_grad


def solution(mesh):
    x_y_half = (4, 4, 2)
    fine = Mesh(mesh.devices.reshape(*x_y_half, -1), ("x", "y", "half", "grp"))
    split = P(("x", "y", "half", "grp"), None)
    return jax.shard_map(
        local, mesh=fine, in_specs=(split, split, P(), P()), out_specs=(split, split, P(), P()), check_vma=False
    )
```

```python
import jax
import jax.numpy as jnp
from jax import lax
from jax.experimental import pallas as pl
from jax.experimental.pallas import tpu as pltpu
from jax.sharding import Mesh
from jax.sharding import PartitionSpec as P

F32, BF16 = jnp.float32, jnp.bfloat16
VMEM = pl.BlockSpec(memory_space=pltpu.VMEM)
SMEM = pl.BlockSpec(memory_space=pltpu.SMEM)
PARAMS = pltpu.CompilerParams(vmem_limit_bytes=48 * 1024 * 1024)


def dot(left, right, left_dim, right_dim):
    return lax.dot_general(
        left, right, (((left_dim,), (right_dim,)), ((), ())), preferred_element_type=F32
    )


def fold(tile):
    return jnp.sum(tile.reshape(-1, 8, tile.shape[-1]), axis=0)


def score(scalars, texts, images, on_diagonal):
    products = dot(texts, images, 1, 1)
    slopes = jax.nn.sigmoid(scalars[0] * products + scalars[1])
    if on_diagonal:
        rows = lax.broadcasted_iota(jnp.int32, slopes.shape, 0)
        columns = lax.broadcasted_iota(jnp.int32, slopes.shape, 1)
        slopes = slopes - jnp.where(rows == columns, 1.0, 0.0)
    return slopes.astype(BF16), fold(slopes), fold(slopes * products)


def first_kernel(scalars, texts, mine, slopes_out, grad_out, sums_out):
    half, bias_sum, scale_sum = score(scalars, texts[...], mine[...], True)
    slopes_out[...] = half
    grad_out[...] = dot(half, mine[...], 1, 0)
    sums_out[0:8] = bias_sum
    sums_out[8:16] = scale_sum


def own_kernel(first_grad, own_slopes, ahead, behind, outer, inner, grad_out):
    grad = first_grad[...]
    for slot, images in enumerate((ahead, behind, outer, inner)):
        grad = grad + dot(own_slopes[slot], images[...], 1, 0)
    grad_out[...] = grad


def lane_row(bias_sum, scale_sum):
    lane = lax.broadcasted_iota(jnp.int32, (1, 128), 1)
    return jnp.where(lane == 0, bias_sum, jnp.where(lane == 1, scale_sum, 0.0))


def far_kernel(scalars, texts, mine, ahead, behind, outer, sums, slopes_out, grad_out, sums_out):
    bias_sum, scale_sum, grad = sums[0:8], sums[8:16], None
    for slot, images in enumerate((mine, ahead, behind, outer)):
        half, bias_part, scale_part = score(scalars, texts[...], images[...], False)
        part = dot(half, images[...], 1, 0)
        grad = part if grad is None else grad + part
        bias_sum, scale_sum = bias_sum + bias_part, scale_sum + scale_part
        slopes_out[slot] = half
    grad_out[...] = grad.astype(BF16)
    sums_out[0:8] = bias_sum
    sums_out[8:16] = scale_sum


def images_kernel(
    scalars, texts, ahead, behind, outer, inner, sums, first_slopes, far_texts, far_slopes, own_out, row_out, *outs
):
    bias_sum, scale_sum = sums[0:8], sums[8:16]
    near = (None, ahead, behind, outer, inner)
    for slot in (3, 4, 1, 2, 0):
        if slot == 0:
            half = first_slopes[...]
        else:
            half, bias_part, scale_part = score(scalars, texts[...], near[slot][...], False)
            bias_sum, scale_sum = bias_sum + bias_part, scale_sum + scale_part
            own_out[slot - 1] = half
        grad = dot(half, texts[...], 0, 0)
        if slot < 4:
            grad = grad + dot(far_slopes[slot], far_texts[...], 0, 0)
        outs[slot][...] = grad.astype(outs[slot].dtype)
    row_out[...] = jnp.broadcast_to(lane_row(jnp.sum(bias_sum), jnp.sum(scale_sum)), row_out.shape)


def column_kernel(rows, *refs):
    refs[-1][...] = jnp.broadcast_to(jnp.sum(rows[...], axis=0, keepdims=True), refs[-1].shape)


def shape(rows, columns, kind):
    return jax.ShapeDtypeStruct((rows, columns), kind)


def cost(moved):
    return pl.CostEstimate(flops=0, bytes_accessed=moved, transcendentals=0)


def call(kernel, name, outs, in_smem, args, moved):
    return pl.pallas_call(
        kernel,
        out_shape=outs,
        in_specs=[SMEM] * in_smem + [VMEM] * (len(args) - in_smem),
        out_specs=(VMEM,) * len(outs),
        compiler_params=PARAMS,
        cost_estimate=pl.CostEstimate(flops=0, bytes_accessed=moved, transcendentals=0),
        name=name,
    )(*args)


def local(images, texts, log_temp, bias):
    rows, width = images.shape
    columns_count, halves = lax.axis_size(("x", "y")), lax.axis_size("half")
    in_column = halves * lax.axis_size("grp")
    stops = columns_count * halves
    scale = jnp.exp(log_temp[0])
    scalars = jnp.stack([scale, bias[0]])
    block = rows * width * 2

    def moved(value, pairs):
        return lax.ppermute(value, ("x", "y", "half"), pairs)

    def columns(count):
        return [(s, (s - 2 * count) % stops) for s in range(stops)]

    def back(pairs):
        return [(b, a) for a, b in pairs]

    flip = [(s, s ^ 1) for s in range(stops)]
    outward = [(s, (s - 4 * (1 - 2 * (s % 2))) % stops) for s in range(stops)]
    ways = (columns(1), columns(-1), outward, back(outward))

    far_texts = moved(texts, flip)
    ahead, behind, outer, inner = [moved(images, way) for way in ways]
    first_slopes, text_first, sums = call(
        first_kernel,
        "first_pair",
        (shape(rows, rows, BF16), shape(rows, width, F32), shape(16, rows, F32)),
        1,
        (scalars, texts, images),
        100 * block,
    )
    far_texts, outer, ahead, behind = lax.optimization_barrier((far_texts, outer, ahead, behind))
    near = (ahead, behind, outer, inner)
    far_slopes, far_grad, sums = call(
        far_kernel,
        "far_pairs",
        (jax.ShapeDtypeStruct((4, rows, rows), BF16), shape(rows, width, BF16), shape(16, rows, F32)),
        1,
        (scalars, far_texts, images, *near[:3], sums),
        block,
    )
    text_back = moved(far_grad, flip)
    own_slopes, row_copies, image_own, *image_parts = call(
        images_kernel,
        "image_parts",
        (jax.ShapeDtypeStruct((4, rows, rows), BF16), shape(in_column, 128, F32), shape(rows, width, F32))
        + (shape(rows, width, BF16),) * 4,
        1,
        (scalars, texts, *near, sums, first_slopes, far_texts, far_slopes),
        block,
    )
    image_back = [moved(part, back(way)) for part, way in zip(image_parts, ways, strict=True)]
    own_slopes, text_first, image_own = lax.optimization_barrier((own_slopes, text_first, image_own))
    (text_own,) = call(
        own_kernel, "own_texts", (shape(rows, width, F32),), 0, (text_first, own_slopes, *near), block
    )
    row_copies, text_own = lax.optimization_barrier((row_copies, text_own))
    column_rows = lax.all_to_all(row_copies, ("half", "grp"), 0, 0, tiled=True)
    row_copies = pl.pallas_call(
        column_kernel,
        out_shape=shape(columns_count, 128, F32),
        in_specs=[VMEM] * 3,
        out_specs=VMEM,
        compiler_params=PARAMS,
        name="column_sums",
    )(column_rows, text_back, image_back[1])
    sums_all = jnp.sum(lax.all_to_all(row_copies, ("x", "y"), 0, 0, tiled=True), axis=0)

    batch_rows = rows * columns_count * in_column
    bias_grad = (sums_all[0] / batch_rows).reshape(1)
    temp_grad = (scale * sums_all[1] / batch_rows).reshape(1)
    image_sum = image_own
    for part in image_back:
        image_sum = image_sum + part.astype(F32)
    text_grad = (scale * (text_own + text_back.astype(F32))).astype(BF16)
    image_grad = (scale * image_sum).astype(BF16)
    return image_grad, text_grad, bias_grad, temp_grad


def solution(mesh):
    x_y_half = (4, 4, 2)
    fine = Mesh(mesh.devices.reshape(*x_y_half, -1), ("x", "y", "half", "grp"))
    split = P(("x", "y", "half", "grp"), None)
    return jax.shard_map(
        local, mesh=fine, in_specs=(split, split, P(), P()), out_specs=(split, split, P(), P()), check_vma=False
    )
```
